256 devices in a mesh: vocab: 32 (over y, z_hi, x), width: 8 (over z_lo, core).
Axes of the slice: x: 4, y: 4, z: 8 (z_hi: 2, z_lo: 4; z = z_hi * 4 + z_lo), core: 2. Of those that a mesh axis runs over, the one named last changes fastest.
Arguments:
- grad_rows: bfloat16 [8192, 5376], P('vocab', 'width'), may hold values from -6 to 6
- eigen_cols: bfloat16 [5376, 5376], P(None, 'width'), may hold values from -0.078125 to 0.078125
- first_moment: float32 [8192, 5376], P('vocab', 'width'), may hold values from -4 to 4
- second_moment: float32 [8192, 5376], P('vocab', 'width'), may hold values from 0.01 to 1
- params: bfloat16 [8192, 5376], P('vocab', 'width'), may hold values from -4 to 4
- covariance: float32 [5376, 5376], P('vocab', 'width'), may hold values from -6 to 6
Outputs:
- params_new: bfloat16 [8192, 5376], P('vocab', 'width')
- first_new: float32 [8192, 5376], P('vocab', 'width')
- second_new: float32 [8192, 5376], P('vocab', 'width')
- covariance_new: float32 [5376, 5376], P('vocab', 'width')
The draws below stay inside these ranges and needn't reach their ends.
All inputs are finite; a program needn't handle non-finite values.
Results may differ from the reference program's by a relative error of at most 0.014.
Values may be sent and summed in bfloat16 or wider, within the bound.
No kernel may reach another device: no remote copies, remote signals or barrier semaphores. Data moves between devices by JAX's collectives and lax.ppermute only.
A program may use at most 128 MiB of HBM per device.

```python
import math
import jax
import jax.numpy as jnp
from jax import lax

D = 5376
VOCAB = 8192


def strengthened(array, key, source, target, shards_of, factor):
    def block_of(axis_at):
        return (jnp.arange(array.shape[axis_at]) // (array.shape[axis_at] // shards_of)).reshape((-1,) + (1,) * (array.ndim - 1 - axis_at))

    first = jax.random.permutation(key, shards_of)[block_of(target)]
    far = (block_of(target) + shards_of // 2) % shards_of
    return jnp.where((block_of(source) == first) | (block_of(source) == far), factor * array, array)


def block_levels(stream_key, shape, pieces, smallest, top_value):
    def one(dim, blocks):
        draws = jax.random.uniform(jax.random.fold_in(jax.random.fold_in(stream_key, 6), dim), (blocks,), jnp.float32, smallest / len(pieces), top_value / len(pieces))
        return jnp.repeat(jnp.exp(draws), shape[dim] // blocks).reshape((-1,) + (1,) * (len(shape) - dim - 1))

    level = one(*pieces[0])
    for cut in pieces[1:]:
        level = level * one(*cut)
    return level


def normal_values(own_key, shape, scale, limit, cuts=(), dtype=jnp.bfloat16):
    drawn = jax.random.normal(own_key, shape, jnp.float32) * scale
    if len(cuts) > 0:
        drawn = block_levels(own_key, shape, cuts, -0.22, 0.18) * drawn
    return jnp.clip(drawn, min=-limit, max=limit).astype(dtype)


def heavy_noise(rng, dims, spread, bound, pieces, heavy, held_as=jnp.bfloat16):
    entries = spread * jax.random.normal(rng, dims, jnp.float32)
    if pieces:
        entries = entries * block_levels(rng, dims, pieces, -0.22, 0.18)
    return jnp.clip(strengthened(entries, jax.random.fold_in(rng, 3), *heavy), -bound, bound).astype(held_as)


def setup_inputs(seed: int = 0) -> dict:
    streams_of = jax.random.split(jax.random.key(seed), 7)
    grad_rows = heavy_noise(streams_of[0], (VOCAB, D), 1.0, 6.0, ((0, 32), (1, 8)), (0, 1, 32, 2.75))
    eigen_cols = normal_values(streams_of[1], (D, D), D ** -0.5, 0.078125, ((1, 8),))
    first_moment = normal_values(streams_of[2], (VOCAB, D), 0.5, 4.0, ((0, 32), (1, 8)), jnp.float32)
    second_moment = jnp.clip(jnp.exp(math.log(1.0) - 4.6051702 * jax.random.uniform(streams_of[3], (VOCAB, D), jnp.float32) ** block_levels(streams_of[3], (VOCAB, D), ((0, 32), (1, 8)), -0.2, 0.2)), 0.01, 1.0)
    params = normal_values(streams_of[4], (VOCAB, D), 0.5, 4.0, ((0, 32), (1, 8)))
    covariance = normal_values(streams_of[5], (D, D), 1.0, 6.0, ((0, 32), (1, 8)), jnp.float32)
    return {"grad_rows": grad_rows, "eigen_cols": eigen_cols, "first_moment": first_moment, "second_moment": second_moment, "params": params, "covariance": covariance}


BIAS_ONE = 1.0 - 0.9 ** 10
BIAS_TWO = 1.0 - 0.95 ** 10

def reference(grad_rows, eigen_cols, first_moment, second_moment, params, covariance):
    rotated = jnp.dot(grad_rows, eigen_cols, preferred_element_type=jnp.float32)
    first_new = 0.9 * first_moment + 0.1 * rotated
    second_new = 0.95 * second_moment + 0.05 * rotated * rotated
    direction = (first_new / BIAS_ONE / (jnp.sqrt(second_new / BIAS_TWO) + 1e-08)).astype(jnp.bfloat16)
    back = lax.dot_general(direction, eigen_cols, (((1,), (1,)), ((), ())), preferred_element_type=jnp.float32)
    params_new = (params.astype(jnp.float32) - 0.25 * back).astype(jnp.bfloat16)
    gram = lax.dot_general(grad_rows, grad_rows, (((0,), (0,)), ((), ())), preferred_element_type=jnp.float32)
    covariance_new = 0.95 * covariance + gram * (1.0 / math.sqrt(VOCAB))
    return (params_new, first_new, second_new, covariance_new)
```

```python
import math

import jax
import jax.numpy as jnp
from jax import lax
from jax.sharding import Mesh, PartitionSpec as P

BIAS_ONE = 1.0 - 0.9**10
BIAS_TWO = 1.0 - 0.95**10
BF16 = jnp.bfloat16
F32 = jnp.float32


def shift(a, axis, n, k):
    return lax.ppermute(a, axis, [(i, (i + k) % n) for i in range(n)])


def flip(a, axis, n, k):
    return lax.ppermute(a, axis, [(i, i ^ k) for i in range(n)])


def local(grad_rows, eigen_cols, first_moment, second_moment, params, covariance):
    x, y = lax.axis_index("x"), lax.axis_index("y")
    h, z, c = lax.axis_index("zh"), lax.axis_index("zl"), lax.axis_index("c")
    nx = lax.axis_size("x")
    vocab_total = grad_rows.shape[0] * lax.axis_size("y") * lax.axis_size("zh") * nx

    g = grad_rows.T
    cols, rows = g.shape
    strip = cols // nx

    across = [g] + [flip(g, "zl", 4, k) for k in (1, 2, 3)]
    own_x = [g] + [shift(g, "x", 4, k) for k in (1, 2, 3)]
    own_y = [g] + [shift(g, "y", 4, k) for k in (1, 2, 3)]
    mine = jnp.stack(across)
    other = flip(mine, "c", 2, 1)
    full = jnp.zeros((4, 2, cols, rows), BF16)
    for k in range(4):
        full = lax.dynamic_update_slice(full, mine[k][None, None], (z ^ k, c, 0, 0))
        full = lax.dynamic_update_slice(full, other[k][None, None], (z ^ k, 1 - c, 0, 0))
    flat = full.reshape(8 * cols, rows)

    by_strip = full[:, 0].reshape(4, nx, strip, rows)
    by_block = full[:, 1]
    ax, by = [], []
    for d in (1, 2, 3):
        part = lax.dynamic_slice(by_strip, (2 * c, (x + d) % 4, 0, 0), (2, 1, strip, rows))
        ax.append(shift(part[:, 0], "x", 4, d))
        part = lax.dynamic_slice(by_block, ((y + d) % 4, c * (cols // 2), 0), (1, cols // 2, rows))
        by.append(shift(part[0], "y", 4, d))
    ax = jnp.stack(ax)
    by = jnp.stack(by)
    ax_other = flip(ax, "c", 2, 1)
    by_other = flip(by, "c", 2, 1)
    ax_low = jnp.where(c == 0, ax, ax_other)
    ax_high = jnp.where(c == 0, ax_other, ax)
    by_low = jnp.where(c == 0, by, by_other)
    by_high = jnp.where(c == 0, by_other, by)
    strips = [lax.dynamic_slice(by_strip, (0, x, 0, 0), (4, 1, strip, rows)).reshape(cols, rows)]
    blocks = [lax.dynamic_slice(by_block, (y, 0, 0), (1, cols, rows))[0]]
    for d in range(3):
        strips.append(jnp.concatenate([ax_low[d], ax_high[d]]).reshape(cols, rows))
        blocks.append(jnp.concatenate([by_low[d], by_high[d]]))

    def products(left, right):
        return lax.dot_general(
            jnp.concatenate(left, axis=1),
            jnp.concatenate(right, axis=1),
            (((1,), (1,)), ((), ())),
            preferred_element_type=F32,
        ).astype(BF16)

    part_a = products(strips, own_x).reshape(4, strip, cols)
    part_b = products(blocks, own_y).reshape(4, strip, cols)

    def scatter(part, me, axis):
        total = lax.dynamic_slice(part, (me, 0, 0), (1, strip, cols))[0].astype(F32)
        got = []
        for d in (1, 2, 3):
            piece = lax.dynamic_slice(part, ((me + d) % 4, 0, 0), (1, strip, cols))[0]
            got.append(shift(piece, axis, 4, d))
        for piece in got:
            total = total + piece.astype(F32)
        return total

    sum_a = scatter(part_a, y, "y")
    sum_b = scatter(part_b, x, "x")
    give = jnp.where(h == 0, sum_b, sum_a).astype(BF16)
    gram = jnp.where(h == 0, sum_a, sum_b) + flip(give, "zh", 2, 1).astype(F32)
    covariance_new = 0.95 * covariance + gram * (1.0 / math.sqrt(vocab_total))

    rotated = lax.dot_general(
        eigen_cols, flat, (((0,), (0,)), ((), ())), preferred_element_type=F32
    )
    first_new = 0.9 * first_moment.T + 0.1 * rotated
    second_new = 0.95 * second_moment.T + 0.05 * rotated * rotated
    direction = (first_new / BIAS_ONE / (jnp.sqrt(second_new / BIAS_TWO) + 1e-08)).astype(BF16)
    back = lax.dot_general(
        eigen_cols, direction, (((1,), (0,)), ((), ())), preferred_element_type=F32
    ).astype(BF16).reshape(4, 2, cols, rows)
    keep = lax.dynamic_index_in_dim(back, c, 1, keepdims=False)
    send = lax.dynamic_index_in_dim(back, 1 - c, 1, keepdims=False)
    both = keep.astype(F32) + flip(send, "c", 2, 1).astype(F32)
    both16 = both.astype(BF16)
    total = lax.dynamic_index_in_dim(both, z, 0, keepdims=False)
    got = []
    for k in (1, 2, 3):
        piece = lax.dynamic_index_in_dim(both16, z ^ k, 0, keepdims=False)
        got.append(flip(piece, "zl", 4, k))
    for piece in got:
        total = total + piece.astype(F32)
    params_new = (params.T.astype(F32) - 0.25 * total).astype(BF16)
    return (params_new.T, first_new.T, second_new.T, covariance_new)


def solution(mesh):
    fine = Mesh(mesh.devices.reshape(4, 2, 4, 4, 2), ("y", "zh", "x", "zl", "c"))
    spec = P(("y", "zh", "x"), ("zl", "c"))
    return jax.shard_map(
        local,
        mesh=fine,
        in_specs=(spec, P(None, ("zl", "c")), spec, spec, spec, spec),
        out_specs=(spec, spec, spec, spec),
        check_vma=False,
    )
```

```python
import math

import jax
import jax.numpy as jnp
import numpy as np
from jax import lax
from jax.experimental import pallas as pl
from jax.experimental.pallas import tpu as pltpu
from jax.sharding import Mesh, PartitionSpec as P

BIAS_ONE = 1.0 - 0.9**10
BIAS_TWO = 1.0 - 0.95**10
BF16 = jnp.bfloat16
F32 = jnp.float32
COST_A = 20_000_000_000
COST_M = 20_000_000_000
COST_F = 20_000_000_000
AXES = ("y", "zh", "x", "zl", "c")
SIZES = (4, 2, 4, 4, 2)
IDS = np.arange(math.prod(SIZES)).reshape(SIZES)
CROSS = [r.tolist() for r in IDS[..., 0].transpose(0, 1, 3, 2).reshape(-1, 4)] + [
    r.tolist() for r in IDS[..., 1].transpose(1, 2, 3, 0).reshape(-1, 4)
]
CROSS_BACK = [r.tolist() for r in IDS[..., 0].transpose(1, 2, 3, 0).reshape(-1, 4)] + [
    r.tolist() for r in IDS[..., 1].transpose(0, 1, 3, 2).reshape(-1, 4)
]


def flip(a, axis, n, k):
    return lax.ppermute(a, axis, [(i, i ^ k) for i in range(n)])


def swap(a, groups):
    return lax.all_to_all(a, AXES, 0, 0, axis_index_groups=groups, tiled=True)


def route(a, target):
    pairs = []
    for i in range(IDS.size):
        to = target(*(int(k) for k in np.unravel_index(i, SIZES)))
        if to is not None:
            pairs.append((i, int(IDS[to])))
    return lax.ppermute(a, AXES, pairs)


def pick(a, i, axis=0):
    return lax.dynamic_index_in_dim(a, i, axis, keepdims=False)


def turn_kernel(a_ref, out_ref):
    out_ref[...] = a_ref[...].T


def turn(a):
    n, m = a.shape
    block = 256
    return pl.pallas_call(
        turn_kernel,
        out_shape=jax.ShapeDtypeStruct((m, n), a.dtype),
        grid=(m // block,),
        in_specs=[pl.BlockSpec((n, block), lambda i: (0, i))],
        out_specs=pl.BlockSpec((block, n), lambda i: (i, 0)),
        compiler_params=pltpu.CompilerParams(vmem_limit_bytes=16 * 2**20),
        cost_estimate=pl.CostEstimate(flops=1, bytes_accessed=1, transcendentals=0),
        name="turn",
    )(a)


def products_kernel(at_ref, l0, l1, l2, l3, early_ref, out_ref):
    me = at_ref[0]
    strip = out_ref.shape[2]
    for w in range(2):
        total = None
        for d, left in enumerate((l0, l1, l2, l3)):
            term = lax.dot_general(
                left[...], early_ref[(me - d + 4) % 4, w],
                (((1,), (1,)), ((), ())), preferred_element_type=F32,
            )
            total = term if total is None else total + term
        for j in range(4):
            out_ref[j, w] = total[j * strip : (j + 1) * strip].astype(BF16)


def products(me, late, early):
    cols = late[0].shape[0]
    vmem = pl.BlockSpec(memory_space=pltpu.VMEM)
    return pl.pallas_call(
        products_kernel,
        out_shape=jax.ShapeDtypeStruct((4, 2, cols // 4, cols), BF16),
        in_specs=[pl.BlockSpec(memory_space=pltpu.SMEM)] + [vmem] * 5,
        out_specs=vmem,
        compiler_params=pltpu.CompilerParams(vmem_limit_bytes=20 * 2**20),
        cost_estimate=pl.CostEstimate(flops=COST_M, bytes_accessed=1, transcendentals=0),
        name="products",
    )(me[None].astype(jnp.int32), *late, early)


def finish_kernel(p_ref, t_ref, a, b, c, out_ref):
    total = t_ref[...] + a[...].astype(F32) + b[...].astype(F32) + c[...].astype(F32)
    out_ref[...] = (p_ref[...].astype(F32) - 0.25 * total).astype(BF16)


def finish(params, total, got):
    vmem = pl.BlockSpec(memory_space=pltpu.VMEM)
    return pl.pallas_call(
        finish_kernel,
        out_shape=jax.ShapeDtypeStruct(params.shape, BF16),
        in_specs=[vmem] * 5,
        out_specs=vmem,
        compiler_params=pltpu.CompilerParams(vmem_limit_bytes=16 * 2**20),
        cost_estimate=pl.CostEstimate(flops=COST_F, bytes_accessed=1, transcendentals=0),
        name="finish",
    )(params, total, *got)


def arrange_kernel(at_ref, g, r1, r2, r3, alike_ref, others_ref):
    z = at_ref[0]
    alike_ref[z] = g[...]
    for k, piece in enumerate((r1, r2, r3)):
        alike_ref[z ^ (k + 1)] = piece[...]
        others_ref[k] = piece[...]


def arrange(z, g, across):
    vmem = pl.BlockSpec(memory_space=pltpu.VMEM)
    return pl.pallas_call(
        arrange_kernel,
        out_shape=(
            jax.ShapeDtypeStruct((4,) + g.shape, BF16),
            jax.ShapeDtypeStruct((3,) + g.shape, BF16),
        ),
        in_specs=[pl.BlockSpec(memory_space=pltpu.SMEM)] + [vmem] * 4,
        out_specs=(vmem, vmem),
        compiler_params=pltpu.CompilerParams(vmem_limit_bytes=16 * 2**20),
        cost_estimate=pl.CostEstimate(flops=COST_A, bytes_accessed=1, transcendentals=0),
        name="arrange",
    )(z[None].astype(jnp.int32), g, *across)


def local(grad_rows, eigen_cols, first_moment, second_moment, params, covariance):
    x, y = lax.axis_index("x"), lax.axis_index("y")
    h, z, c = lax.axis_index("zh"), lax.axis_index("zl"), lax.axis_index("c")
    vocab_total = grad_rows.shape[0] * 32

    g = grad_rows.T
    cols, rows = g.shape
    strip = cols // 4

    with jax.named_scope("early"):
        partner = flip(g, "c", 2, 1)
        across = [flip(g, "zl", 4, k) for k in (1, 2, 3)]
        pair = jnp.where(c == 0, jnp.stack([g, partner]), jnp.stack([partner, g]))
        early = swap(jnp.broadcast_to(pair[None], (4,) + pair.shape), CROSS)
        by_rows = turn(eigen_cols.T)
        alike, others = arrange(z, g, across)
        alike, others, early, by_rows = lax.optimization_barrier((alike, others, early, by_rows))

    with jax.named_scope("late"):
        by_strip = alike.reshape(4, 4, strip, rows)
        late = []
        for d in range(4):
            part = jnp.where(c == 0, pick(by_strip, (x + d) % 4, 1), pick(by_strip, (y + d) % 4, 0))
            if d > 0:
                part = route(
                    part,
                    lambda y, h, x, z, c: (y, h, (x + d) % 4, z, c) if c == 0 else ((y + d) % 4, h, x, z, c),
                )
            late.append(part.reshape(cols, rows))

    with jax.named_scope("cores"):
        other = flip(others, "c", 2, 1)
        full = jnp.zeros((4, 2, cols, rows), BF16)
        full = lax.dynamic_update_slice(full, alike[:, None], (0, c, 0, 0))
        full = lax.dynamic_update_slice(full, partner[None, None], (z, 1 - c, 0, 0))
        for k in (1, 2, 3):
            full = lax.dynamic_update_slice(full, other[k - 1][None, None], (z ^ k, 1 - c, 0, 0))
        flat = full.reshape(8 * cols, rows)

    with jax.named_scope("rotated"):
        rotated = lax.dot_general(
            eigen_cols, flat, (((0,), (0,)), ((), ())), preferred_element_type=F32
        )
        first_new = 0.9 * first_moment.T + 0.1 * rotated
        second_new = 0.95 * second_moment.T + 0.05 * rotated * rotated
        direction = (
            first_new / BIAS_ONE / (jnp.sqrt(second_new / BIAS_TWO) + 1e-08)
        ).astype(BF16)
        back = lax.dot_general(
            by_rows, direction, (((1,), (0,)), ((), ())), preferred_element_type=F32
        ).astype(BF16).reshape(4, 2, cols, rows)
        send = pick(back, 1 - c, 1)
        both = pick(back, c, 1).astype(F32) + flip(send, "c", 2, 1).astype(F32)
        both16 = both.astype(BF16)

    with jax.named_scope("gram"):
        part = products(jnp.where(c == 0, x, y), late, early)
        part, both16 = lax.optimization_barrier((part, both16))
        got = [flip(pick(both16, z ^ k), "zl", 4, k) for k in (1, 2, 3)]
        total = pick(both, z)
        gram = jnp.sum(swap(part, CROSS_BACK).astype(F32), 0)

    with jax.named_scope("finish"):
        params_new = finish(params.T, total, got)
        same = pick(gram, c)
        gram16 = gram.astype(BF16)
        to_other, to_same = pick(gram16, 1 - c), pick(gram16, c)
        near = route(to_other, lambda y, h, x, z, c: (y, h, x, z, 1 - c) if c == h else None)
        far = route(to_other, lambda y, h, x, z, c: (y, 1 - h, x, z, 1 - c) if c != h else None)
        far2 = route(to_same, lambda y, h, x, z, c: (y, 1 - h, x, z, c) if c != h else None)
        gram = jnp.where(c == h, same, near.astype(F32)) + jnp.where(c == h, far2, far).astype(F32)
        covariance_new = 0.95 * covariance + gram * (1.0 / math.sqrt(vocab_total))
    return (params_new.T, first_new.T, second_new.T, covariance_new)


def solution(mesh):
    fine = Mesh(mesh.devices.reshape(SIZES), AXES)
    spec = P(("y", "zh", "x"), ("zl", "c"))
    return jax.shard_map(
        local,
        mesh=fine,
        in_specs=(spec, P(None, ("zl", "c")), spec, spec, spec, spec),
        out_specs=(spec, spec, spec, spec),
        check_vma=False,
    )
```

```python
import math

import jax
import jax.numpy as jnp
import numpy as np
from jax import lax
from jax.experimental import pallas as pl
from jax.experimental.pallas import tpu as pltpu
from jax.sharding import Mesh, PartitionSpec as P

BIAS_ONE = 1.0 - 0.9**10
BIAS_TWO = 1.0 - 0.95**10
BF16 = jnp.bfloat16
F32 = jnp.float32
COST_A = 16_000_000_000
COST_M = 11_000_000_000
COST_G = 1
COST_B = 10_000_000_000
COST_R = 10_000_000_000
COST_T = 1
COST_F = 20_000_000_000
AXES = ("y", "zh", "x", "zl", "c")
SIZES = (4, 2, 4, 4, 2)
IDS = np.arange(math.prod(SIZES)).reshape(SIZES)
CROSS = [r.tolist() for r in IDS[..., 0].transpose(0, 1, 3, 2).reshape(-1, 4)] + [
    r.tolist() for r in IDS[..., 1].transpose(1, 2, 3, 0).reshape(-1, 4)
]
CROSS_BACK = [r.tolist() for r in IDS[..., 0].transpose(1, 2, 3, 0).reshape(-1, 4)] + [
    r.tolist() for r in IDS[..., 1].transpose(0, 1, 3, 2).reshape(-1, 4)
]


def flip(a, axis, n, k):
    return lax.ppermute(a, axis, [(i, i ^ k) for i in range(n)])


def swap(a, groups):
    return lax.all_to_all(a, AXES, 0, 0, axis_index_groups=groups, tiled=True)


def route(a, target):
    pairs = []
    for i in range(IDS.size):
        to = target(*(int(k) for k in np.unravel_index(i, SIZES)))
        if to is not None:
            pairs.append((i, int(IDS[to])))
    return lax.ppermute(a, AXES, pairs)


def index(*at):
    return jnp.stack(at).astype(jnp.int32)


def pick(a, i, axis=0):
    return lax.dynamic_index_in_dim(a, i, axis, keepdims=False)


def spec(space=pltpu.VMEM):
    return pl.BlockSpec(memory_space=space)


def call(kernel, name, flops, out_shape, n_in, scratch=(), limit=8):
    return pl.pallas_call(
        kernel,
        out_shape=out_shape,
        in_specs=[spec(pltpu.SMEM)] + [spec()] * n_in,
        out_specs=jax.tree.map(lambda _: spec(), out_shape),
        scratch_shapes=scratch,
        compiler_params=pltpu.CompilerParams(vmem_limit_bytes=limit * 2**20),
        cost_estimate=pl.CostEstimate(flops=flops, bytes_accessed=1, transcendentals=0),
        name=name,
    )


def turn_kernel(a_ref, out_ref):
    out_ref[...] = a_ref[...].T


def turn(a):
    n, m = a.shape
    block = 1792
    return pl.pallas_call(
        turn_kernel,
        out_shape=jax.ShapeDtypeStruct((m, n), a.dtype),
        grid=(m // block,),
        in_specs=[pl.BlockSpec((n, block), lambda i: (0, i))],
        out_specs=pl.BlockSpec((block, n), lambda i: (i, 0)),
        compiler_params=pltpu.CompilerParams(vmem_limit_bytes=46 * 2**20),
        cost_estimate=pl.CostEstimate(flops=COST_T, bytes_accessed=1, transcendentals=0),
        name="turn",
    )(a)


def products_kernel(at_ref, l0, l1, l2, l3, early_ref, o0, o1, o2, o3, held):
    me, to = at_ref[0], at_ref[1]
    strip = held.shape[1]
    left = jnp.concatenate([l0[...], l1[...], l2[...], l3[...]], axis=1)
    for w in range(2):
        right = jnp.concatenate([early_ref[(me - d + 4) % 4, w] for d in range(4)], axis=1)
        total = lax.dot_general(
            left, right, (((1,), (1,)), ((), ())), preferred_element_type=F32
        )
        for j in range(4):
            held[j] = total[j * strip : (j + 1) * strip]
        for d, out in enumerate((o0, o1, o2, o3)):
            out[w] = held[(to + d) % 4].astype(BF16)


def products(at, late, early):
    cols = late[0].shape[0]
    out = jax.ShapeDtypeStruct((2, cols // 4, cols), BF16)
    held = pltpu.VMEM((4, cols // 4, cols), F32)
    return call(products_kernel, "products", COST_M, (out,) * 4, 5, [held], limit=20)(at, *late, early)


def add_kernel(at_ref, back_ref, got_ref, own_ref, *outs):
    c, z = at_ref[0], at_ref[1]
    total = [None] * 4
    for k in range(4):
        to = z ^ k
        value = back_ref[to, c].astype(F32) + got_ref[to].astype(F32)
        if k == 0:
            own_ref[...] = value
        else:
            outs[k - 1][...] = value.astype(BF16)


def add(at, back, got):
    shape = got.shape[1:]
    out = (jax.ShapeDtypeStruct(shape, F32),) + (jax.ShapeDtypeStruct(shape, BF16),) * 3
    return call(add_kernel, "add", 1, out, 2)(at, back, got)


def fold_kernel(at_ref, a, b, c, d, same_ref, other_ref):
    first = at_ref[0] == 0
    even = sum(r[0].astype(F32) for r in (a, b, c, d))
    odd = sum(r[1].astype(F32) for r in (a, b, c, d))
    same_ref[...] = jnp.where(first, even, odd)
    other_ref[...] = jnp.where(first, odd, even).astype(BF16)


def fold(at, parts):
    shape = parts[0].shape[1:]
    out = (jax.ShapeDtypeStruct(shape, F32), jax.ShapeDtypeStruct(shape, BF16))
    return call(fold_kernel, "fold", COST_G, out, 4)(at, *parts)


def choose_kernel(at_ref, same_ref, near_ref, keep_ref, give_ref):
    stays = at_ref[0] == at_ref[1]
    same, near = same_ref[...], near_ref[...].astype(F32)
    keep_ref[...] = jnp.where(stays, same, near)
    give_ref[...] = jnp.where(stays, near, same).astype(BF16)


def choose(at, same, near):
    out = (jax.ShapeDtypeStruct(same.shape, F32), jax.ShapeDtypeStruct(same.shape, BF16))
    return call(choose_kernel, "choose", COST_G, out, 2)(at, same, near)


def relay_kernel(at_ref, a, b, out_ref):
    out_ref[...] = (a[...].astype(F32) + b[...].astype(F32)).astype(BF16)


def relay(at, a, b):
    return call(relay_kernel, "relay", COST_R, jax.ShapeDtypeStruct(a.shape, BF16), 2)(at, a, b)


def finish_kernel(at_ref, p_ref, own, a, b, c, out_ref):
    total = own[...] + a[...].astype(F32) + b[...].astype(F32) + c[...].astype(F32)
    out_ref[...] = (p_ref[...].astype(F32) - 0.25 * total).astype(BF16)


def finish(at, params, pieces):
    out = jax.ShapeDtypeStruct(params.shape, BF16)
    return call(finish_kernel, "finish", COST_F, out, 5)(at, params, *pieces)


def gather_kernel(at_ref, alike, partner, o1, o2, o3, out_ref):
    z, c = at_ref[0], at_ref[1]
    for k in range(4):
        out_ref[k, c] = alike[k]
    for k, piece in enumerate((partner, o1, o2, o3)):
        out_ref[z ^ k, 1 - c] = piece[...]


def gather(at, alike, other):
    out = jax.ShapeDtypeStruct((4, 2) + alike.shape[1:], BF16)
    return call(gather_kernel, "gather", COST_B, out, 5)(at, alike, *other)


def arrange_kernel(at_ref, g, r1, r2, middle, edge, alike_ref, last_ref):
    z = at_ref[0]
    last = jnp.where((z == 1) | (z == 2), middle[...], edge[...])
    last_ref[...] = last
    alike_ref[z] = g[...]
    alike_ref[z ^ 1] = r1[...]
    alike_ref[z ^ 2] = r2[...]
    alike_ref[z ^ 3] = last


def arrange(at, pieces):
    shape = pieces[0].shape
    out = (jax.ShapeDtypeStruct((4,) + shape, BF16), jax.ShapeDtypeStruct(shape, BF16))
    return call(arrange_kernel, "arrange", COST_A, out, 5)(at, *pieces)


def local(grad_rows, eigen_cols, first_moment, second_moment, params, covariance):
    x, y = lax.axis_index("x"), lax.axis_index("y")
    h, z, c = lax.axis_index("zh"), lax.axis_index("zl"), lax.axis_index("c")
    vocab_total = grad_rows.shape[0] * 32

    g = grad_rows.T
    cols, rows = g.shape
    strip = cols // 4

    with jax.named_scope("early"):
        partner = flip(g, "c", 2, 1)
        across = [flip(g, "zl", 4, k) for k in (1, 2)]
        pair = jnp.where(c == 0, jnp.stack([g, partner]), jnp.stack([partner, g]))
        early = swap(jnp.broadcast_to(pair[None], (4,) + pair.shape), CROSS)
        by_rows = turn(eigen_cols.T)
        *across, g_after, by_rows = lax.optimization_barrier((*across, g, by_rows))
        middle = lax.ppermute(g_after, "zl", [(1, 2), (2, 1)])
        edge = lax.ppermute(across[1], "zl", [(1, 0), (2, 3)])
        alike, last = arrange(index(z), [g, *across, middle, edge])
        other = [partner] + [flip(piece, "c", 2, 1) for piece in across]
        alike, last, other, early, by_rows = lax.optimization_barrier((alike, last, other, early, by_rows))

    with jax.named_scope("late"):
        by_strip = alike.reshape(4, 4, strip, rows)
        late = []
        for d in range(4):
            part = jnp.where(c == 0, pick(by_strip, (x + d) % 4, 1), pick(by_strip, (y + d) % 4, 0))
            if d > 0:
                part = route(
                    part,
                    lambda y, h, x, z, c: (y, h, (x + d) % 4, z, c) if c == 0 else ((y + d) % 4, h, x, z, c),
                )
            late.append(part.reshape(cols, rows))

    with jax.named_scope("cores"):
        other = other + [flip(last, "c", 2, 1)]
        full = gather(index(z, c), alike, other)
        flat = full.reshape(8 * cols, rows)

    with jax.named_scope("rotated"):
        rotated = lax.dot_general(
            eigen_cols, flat, (((0,), (0,)), ((), ())), preferred_element_type=F32
        )
        first_new = 0.9 * first_moment.T + 0.1 * rotated
        second_new = 0.95 * second_moment.T + 0.05 * rotated * rotated
        direction = (
            first_new / BIAS_ONE / (jnp.sqrt(second_new / BIAS_TWO) + 1e-08)
        ).astype(BF16)
        back = lax.dot_general(
            by_rows, direction, (((1,), (0,)), ((), ())), preferred_element_type=F32
        ).astype(BF16).reshape(4, 2, cols, rows)
        send = pick(back, 1 - c, 1)
        own, *both = add(index(c, z), back, flip(send, "c", 2, 1))

    with jax.named_scope("gram"):
        parts = products(index(jnp.where(c == 0, x, y), jnp.where(c == 0, y, x)), late, early)
        parts, both = lax.optimization_barrier((list(parts), both))

    with jax.named_scope("back"):
        one, two, three = both
        passed = lax.ppermute(three, "zl", [(0, 1), (3, 2)])
        middle = lax.ppermute(three, "zl", [(1, 2), (2, 1)])
        one, passed = lax.optimization_barrier((one, passed))
        two = relay(index(z), two, passed)
        got = [own, flip(one, "zl", 4, 1), flip(two, "zl", 4, 2), middle]

    with jax.named_scope("gram"):
        for d in (1, 2, 3):
            parts[d] = route(
                parts[d],
                lambda y, h, x, z, c: ((y + d) % 4, h, x, z, c) if c == 0 else (y, h, (x + d) % 4, z, c),
            )
        same, to_other = fold(index(c), parts)

    with jax.named_scope("finish"):
        params_new = finish(index(c), params.T, got)
        keep, give = choose(index(c, h), same, flip(to_other, "c", 2, 1))
        gram = keep + flip(give, "zh", 2, 1).astype(F32)
        covariance_new = 0.95 * covariance + gram * (1.0 / math.sqrt(vocab_total))
    return (params_new.T, first_new.T, second_new.T, covariance_new)


def solution(mesh):
    fine = Mesh(mesh.devices.reshape(SIZES), AXES)
    spec = P(("y", "zh", "x"), ("zl", "c"))
    return jax.shard_map(
        local,
        mesh=fine,
        in_specs=(spec, P(None, ("zl", "c")), spec, spec, spec, spec),
        out_specs=(spec, spec, spec, spec),
        check_vma=False,
    )
```

```python
import math

import jax
import jax.numpy as jnp
import numpy as np
from jax import lax
from jax.experimental import pallas as pl
from jax.experimental.pallas import tpu as pltpu
from jax.sharding import Mesh, PartitionSpec as P

BIAS_ONE = 1.0 - 0.9**10
BIAS_TWO = 1.0 - 0.95**10
BF16 = jnp.bfloat16
F32 = jnp.float32
COST_A = 16_000_000_000
COST_M = 11_000_000_000
COST_G = 1
COST_B = 10_000_000_000
COST_R = 10_000_000_000
COST_T = 1
COST_F = 20_000_000_000
AXES = ("y", "zh", "x", "zl", "c")
SIZES = (4, 2, 4, 4, 2)
IDS = np.arange(math.prod(SIZES)).reshape(SIZES)
CROSS = [r.tolist() for r in IDS[..., 0].transpose(0, 1, 3, 2).reshape(-1, 4)] + [
    r.tolist() for r in IDS[..., 1].transpose(1, 2, 3, 0).reshape(-1, 4)
]
CROSS_BACK = [r.tolist() for r in IDS[..., 0].transpose(1, 2, 3, 0).reshape(-1, 4)] + [
    r.tolist() for r in IDS[..., 1].transpose(0, 1, 3, 2).reshape(-1, 4)
]


def flip(a, axis, n, k):
    return lax.ppermute(a, axis, [(i, i ^ k) for i in range(n)])


def swap(a, groups):
    return lax.all_to_all(a, AXES, 0, 0, axis_index_groups=groups, tiled=True)


def route(a, target):
    pairs = []
    for i in range(IDS.size):
        to = target(*(int(k) for k in np.unravel_index(i, SIZES)))
        if to is not None:
            pairs.append((i, int(IDS[to])))
    return lax.ppermute(a, AXES, pairs)


def index(*at):
    return jnp.stack(at).astype(jnp.int32)


def pick(a, i, axis=0):
    return lax.dynamic_index_in_dim(a, i, axis, keepdims=False)


def spec(space=pltpu.VMEM):
    return pl.BlockSpec(memory_space=space)


def call(kernel, name, flops, out_shape, n_in, scratch=(), limit=8):
    return pl.pallas_call(
        kernel,
        out_shape=out_shape,
        in_specs=[spec(pltpu.SMEM)] + [spec()] * n_in,
        out_specs=jax.tree.map(lambda _: spec(), out_shape),
        scratch_shapes=scratch,
        compiler_params=pltpu.CompilerParams(vmem_limit_bytes=limit * 2**20),
        cost_estimate=pl.CostEstimate(flops=flops, bytes_accessed=1, transcendentals=0),
        name=name,
    )


def turn_kernel(a_ref, out_ref):
    out_ref[...] = a_ref[...].T


def turn(a):
    n, m = a.shape
    block = 1792
    return pl.pallas_call(
        turn_kernel,
        out_shape=jax.ShapeDtypeStruct((m, n), a.dtype),
        grid=(m // block,),
        in_specs=[pl.BlockSpec((n, block), lambda i: (0, i))],
        out_specs=pl.BlockSpec((block, n), lambda i: (i, 0)),
        compiler_params=pltpu.CompilerParams(vmem_limit_bytes=46 * 2**20),
        cost_estimate=pl.CostEstimate(flops=COST_T, bytes_accessed=1, transcendentals=0),
        name="turn",
    )(a)


def products_kernel(at_ref, l0, l1, l2, l3, early_ref, o0, o1, o2, o3, held):
    me, to = at_ref[0], at_ref[1]
    strip = held.shape[1]
    left = jnp.concatenate([l0[...], l1[...], l2[...], l3[...]], axis=1)
    for w in range(2):
        right = jnp.concatenate([early_ref[(me - d + 4) % 4, w] for d in range(4)], axis=1)
        total = lax.dot_general(
            left, right, (((1,), (1,)), ((), ())), preferred_element_type=F32
        )
        for j in range(4):
            held[j] = total[j * strip : (j + 1) * strip]
        for d, out in enumerate((o0, o1, o2, o3)):
            out[w] = held[(to + d) % 4].astype(BF16)


def products(at, late, early):
    cols = late[0].shape[0]
    out = jax.ShapeDtypeStruct((2, cols // 4, cols), BF16)
    held = pltpu.VMEM((4, cols // 4, cols), F32)
    return call(products_kernel, "products", COST_M, (out,) * 4, 5, [held], limit=20)(at, *late, early)


def add_kernel(at_ref, back_ref, got_ref, own_ref, *outs):
    c, z = at_ref[0], at_ref[1]
    total = [None] * 4
    for k in range(4):
        to = z ^ k
        value = back_ref[to, c].astype(F32) + got_ref[to].astype(F32)
        if k == 0:
            own_ref[...] = value
        else:
            outs[k - 1][...] = value.astype(BF16)


def add(at, back, got):
    shape = got.shape[1:]
    out = (jax.ShapeDtypeStruct(shape, F32),) + (jax.ShapeDtypeStruct(shape, BF16),) * 3
    return call(add_kernel, "add", 1, out, 2)(at, back, got)


def fold_kernel(at_ref, a, b, c, d, same_ref, other_ref):
    first = at_ref[0] == 0
    even = sum(r[0].astype(F32) for r in (a, b, c, d))
    odd = sum(r[1].astype(F32) for r in (a, b, c, d))
    same_ref[...] = jnp.where(first, even, odd)
    other_ref[...] = jnp.where(first, odd, even).astype(BF16)


def fold(at, parts):
    shape = parts[0].shape[1:]
    out = (jax.ShapeDtypeStruct(shape, F32), jax.ShapeDtypeStruct(shape, BF16))
    return call(fold_kernel, "fold", COST_G, out, 4)(at, *parts)


def choose_kernel(at_ref, same_ref, near_ref, keep_ref, give_ref):
    stays = at_ref[0] == at_ref[1]
    same, near = same_ref[...], near_ref[...].astype(F32)
    keep_ref[...] = jnp.where(stays, same, near)
    give_ref[...] = jnp.where(stays, near, same).astype(BF16)


def choose(at, same, near):
    out = (jax.ShapeDtypeStruct(same.shape, F32), jax.ShapeDtypeStruct(same.shape, BF16))
    return call(choose_kernel, "choose", COST_G, out, 2)(at, same, near)


def relay_kernel(at_ref, a, b, out_ref):
    out_ref[...] = (a[...].astype(F32) + b[...].astype(F32)).astype(BF16)


def relay(at, a, b):
    return call(relay_kernel, "relay", COST_R, jax.ShapeDtypeStruct(a.shape, BF16), 2)(at, a, b)


def finish_kernel(at_ref, p_ref, own, a, b, c, out_ref):
    total = own[...] + a[...].astype(F32) + b[...].astype(F32) + c[...].astype(F32)
    out_ref[...] = (p_ref[...].astype(F32) - 0.25 * total).astype(BF16)


def finish(at, params, pieces):
    out = jax.ShapeDtypeStruct(params.shape, BF16)
    return call(finish_kernel, "finish", COST_F, out, 5)(at, params, *pieces)


def gather_kernel(at_ref, alike, partner, o1, o2, o3, out_ref):
    z, c = at_ref[0], at_ref[1]
    for k in range(4):
        out_ref[k, c] = alike[k]
    for k, piece in enumerate((partner, o1, o2, o3)):
        out_ref[z ^ k, 1 - c] = piece[...]


def gather(at, alike, other):
    out = jax.ShapeDtypeStruct((4, 2) + alike.shape[1:], BF16)
    return call(gather_kernel, "gather", COST_B, out, 5)(at, alike, *other)


def arrange_kernel(at_ref, g, r1, r2, middle, edge, alike_ref, last_ref):
    z = at_ref[0]
    last = jnp.where((z == 1) | (z == 2), middle[...], edge[...])
    last_ref[...] = last
    alike_ref[z] = g[...]
    alike_ref[z ^ 1] = r1[...]
    alike_ref[z ^ 2] = r2[...]
    alike_ref[z ^ 3] = last


def arrange(at, pieces):
    shape = pieces[0].shape
    out = (jax.ShapeDtypeStruct((4,) + shape, BF16), jax.ShapeDtypeStruct(shape, BF16))
    return call(arrange_kernel, "arrange", COST_A, out, 5)(at, *pieces)


def local(grad_rows, eigen_cols, first_moment, second_moment, params, covariance):
    x, y = lax.axis_index("x"), lax.axis_index("y")
    h, z, c = lax.axis_index("zh"), lax.axis_index("zl"), lax.axis_index("c")
    vocab_total = grad_rows.shape[0] * 32

    g = grad_rows.T
    cols, rows = g.shape
    strip = cols // 4

    with jax.named_scope("early"):
        partner = flip(g, "c", 2, 1)
        across = [flip(g, "zl", 4, k) for k in (1, 2)]
        pair = jnp.where(c == 0, jnp.stack([g, partner]), jnp.stack([partner, g]))
        early = swap(jnp.broadcast_to(pair[None], (4,) + pair.shape), CROSS)
        by_rows = turn(eigen_cols.T)
        *across, g_after, by_rows = lax.optimization_barrier((*across, g, by_rows))
        middle = lax.ppermute(g_after, "zl", [(1, 2), (2, 1)])
        edge = lax.ppermute(across[1], "zl", [(1, 0), (2, 3)])
        alike, last = arrange(index(z), [g, *across, middle, edge])
        alike, last, early, by_rows = lax.optimization_barrier((alike, last, early, by_rows))

    with jax.named_scope("late"):
        by_strip = alike.reshape(4, 4, strip, rows)
        late = []
        for d in range(4):
            part = jnp.where(c == 0, pick(by_strip, (x + d) % 4, 1), pick(by_strip, (y + d) % 4, 0))
            if d > 0:
                part = route(
                    part,
                    lambda y, h, x, z, c: (y, h, (x + d) % 4, z, c) if c == 0 else ((y + d) % 4, h, x, z, c),
                )
            late.append(part.reshape(cols, rows))

    with jax.named_scope("cores"):
        other = [partner] + [flip(piece, "c", 2, 1) for piece in (*across, last)]
        full = gather(index(z, c), alike, other)
        flat = full.reshape(8 * cols, rows)

    with jax.named_scope("rotated"):
        rotated = lax.dot_general(
            eigen_cols, flat, (((0,), (0,)), ((), ())), preferred_element_type=F32
        )
        first_new = 0.9 * first_moment.T + 0.1 * rotated
        second_new = 0.95 * second_moment.T + 0.05 * rotated * rotated
        direction = (
            first_new / BIAS_ONE / (jnp.sqrt(second_new / BIAS_TWO) + 1e-08)
        ).astype(BF16)
        back = lax.dot_general(
            by_rows, direction, (((1,), (0,)), ((), ())), preferred_element_type=F32
        ).astype(BF16).reshape(4, 2, cols, rows)
        send = pick(back, 1 - c, 1)
        own, *both = add(index(c, z), back, flip(send, "c", 2, 1))

    with jax.named_scope("gram"):
        parts = products(index(jnp.where(c == 0, x, y), jnp.where(c == 0, y, x)), late, early)
        parts, both = lax.optimization_barrier((list(parts), both))

    with jax.named_scope("back"):
        one, two, three = both
        passed = lax.ppermute(three, "zl", [(0, 1), (3, 2)])
        middle = lax.ppermute(three, "zl", [(1, 2), (2, 1)])
        one, passed = lax.optimization_barrier((one, passed))
        two = relay(index(z), two, passed)
        got = [own, flip(one, "zl", 4, 1), flip(two, "zl", 4, 2), middle]

    with jax.named_scope("gram"):
        for d in (1, 2, 3):
            parts[d] = route(
                parts[d],
                lambda y, h, x, z, c: ((y + d) % 4, h, x, z, c) if c == 0 else (y, h, (x + d) % 4, z, c),
            )
        same, to_other = fold(index(c), parts)

    with jax.named_scope("finish"):
        params_new = finish(index(c), params.T, got)
        keep, give = choose(index(c, h), same, flip(to_other, "c", 2, 1))
        gram = keep + flip(give, "zh", 2, 1).astype(F32)
        covariance_new = 0.95 * covariance + gram * (1.0 / math.sqrt(vocab_total))
    return (params_new.T, first_new.T, second_new.T, covariance_new)


def solution(mesh):
    fine = Mesh(mesh.devices.reshape(SIZES), AXES)
    spec = P(("y", "zh", "x"), ("zl", "c"))
    return jax.shard_map(
        local,
        mesh=fine,
        in_specs=(spec, P(None, ("zl", "c")), spec, spec, spec, spec),
        out_specs=(spec, spec, spec, spec),
        check_vma=False,
    )
```

```python
import math

import jax
import jax.numpy as jnp
import numpy as np
from jax import lax
from jax.experimental import pallas as pl
from jax.experimental.pallas import tpu as pltpu
from jax.sharding import Mesh, PartitionSpec as P

BIAS_ONE = 1.0 - 0.9**10
BIAS_TWO = 1.0 - 0.95**10
BF16 = jnp.bfloat16
F32 = jnp.float32
COST_A = 16_000_000_000
COST_M = 11_000_000_000
COST_G = 1
COST_B = 10_000_000_000
COST_R = 10_000_000_000
COST_T = 1
COST_F = 20_000_000_000
AXES = ("y", "zh", "x", "zl", "c")
SIZES = (4, 2, 4, 4, 2)
IDS = np.arange(math.prod(SIZES)).reshape(SIZES)
CROSS = [r.tolist() for r in IDS[..., 0].transpose(0, 1, 3, 2).reshape(-1, 4)] + [
    r.tolist() for r in IDS[..., 1].transpose(1, 2, 3, 0).reshape(-1, 4)
]
CROSS_BACK = [r.tolist() for r in IDS[..., 0].transpose(1, 2, 3, 0).reshape(-1, 4)] + [
    r.tolist() for r in IDS[..., 1].transpose(0, 1, 3, 2).reshape(-1, 4)
]


def flip(a, axis, n, k):
    return lax.ppermute(a, axis, [(i, i ^ k) for i in range(n)])


def swap(a, groups):
    return lax.all_to_all(a, AXES, 0, 0, axis_index_groups=groups, tiled=True)


def route(a, target):
    pairs = []
    for i in range(IDS.size):
        to = target(*(int(k) for k in np.unravel_index(i, SIZES)))
        if to is not None:
            pairs.append((i, int(IDS[to])))
    return lax.ppermute(a, AXES, pairs)


def index(*at):
    return jnp.stack(at).astype(jnp.int32)


def pick(a, i, axis=0):
    return lax.dynamic_index_in_dim(a, i, axis, keepdims=False)


def spec(space=pltpu.VMEM):
    return pl.BlockSpec(memory_space=space)


def call(kernel, name, flops, out_shape, n_in, scratch=(), limit=8):
    return pl.pallas_call(
        kernel,
        out_shape=out_shape,
        in_specs=[spec(pltpu.SMEM)] + [spec()] * n_in,
        out_specs=jax.tree.map(lambda _: spec(), out_shape),
        scratch_shapes=scratch,
        compiler_params=pltpu.CompilerParams(vmem_limit_bytes=limit * 2**20),
        cost_estimate=pl.CostEstimate(flops=flops, bytes_accessed=1, transcendentals=0),
        name=name,
    )


def turn_kernel(a_ref, out_ref):
    out_ref[...] = a_ref[...].T


def turn(a):
    n, m = a.shape
    block = 1792
    return pl.pallas_call(
        turn_kernel,
        out_shape=jax.ShapeDtypeStruct((m, n), a.dtype),
        grid=(m // block,),
        in_specs=[pl.BlockSpec((n, block), lambda i: (0, i))],
        out_specs=pl.BlockSpec((block, n), lambda i: (i, 0)),
        compiler_params=pltpu.CompilerParams(vmem_limit_bytes=46 * 2**20),
        cost_estimate=pl.CostEstimate(flops=COST_T, bytes_accessed=1, transcendentals=0),
        name="turn",
    )(a)


def products_kernel(at_ref, l0, l1, l2, l3, early_ref, o0, o1, o2, o3, held):
    me, to = at_ref[0], at_ref[1]
    strip = held.shape[1]
    left = jnp.concatenate([l0[...], l1[...], l2[...], l3[...]], axis=1)
    for w in range(2):
        right = jnp.concatenate([early_ref[(me - d + 4) % 4, w] for d in range(4)], axis=1)
        total = lax.dot_general(
            left, right, (((1,), (1,)), ((), ())), preferred_element_type=F32
        )
        for j in range(4):
            held[j] = total[j * strip : (j + 1) * strip]
        for d, out in enumerate((o0, o1, o2, o3)):
            out[w] = held[(to + d) % 4].astype(BF16)


def products(at, late, early):
    cols = late[0].shape[0]
    out = jax.ShapeDtypeStruct((2, cols // 4, cols), BF16)
    held = pltpu.VMEM((4, cols // 4, cols), F32)
    return call(products_kernel, "products", COST_M, (out,) * 4, 5, [held], limit=20)(at, *late, early)


def add_kernel(at_ref, back_ref, got_ref, own_ref, *outs):
    c, z = at_ref[0], at_ref[1]
    total = [None] * 4
    for k in range(4):
        to = z ^ k
        value = back_ref[to, c].astype(F32) + got_ref[to].astype(F32)
        if k == 0:
            own_ref[...] = value
        else:
            outs[k - 1][...] = value.astype(BF16)


def add(at, back, got):
    shape = got.shape[1:]
    out = (jax.ShapeDtypeStruct(shape, F32),) + (jax.ShapeDtypeStruct(shape, BF16),) * 3
    return call(add_kernel, "add", 1, out, 2)(at, back, got)


def fold_kernel(at_ref, a, b, c, d, same_ref, other_ref):
    first = at_ref[0] == 0
    even = sum(r[0].astype(F32) for r in (a, b, c, d))
    odd = sum(r[1].astype(F32) for r in (a, b, c, d))
    same_ref[...] = jnp.where(first, even, odd)
    other_ref[...] = jnp.where(first, odd, even).astype(BF16)


def fold(at, parts):
    shape = parts[0].shape[1:]
    out = (jax.ShapeDtypeStruct(shape, F32), jax.ShapeDtypeStruct(shape, BF16))
    return call(fold_kernel, "fold", COST_G, out, 4)(at, *parts)


def choose_kernel(at_ref, same_ref, near_ref, keep_ref, give_ref):
    stays = at_ref[0] == at_ref[1]
    same, near = same_ref[...], near_ref[...].astype(F32)
    keep_ref[...] = jnp.where(stays, same, near)
    give_ref[...] = jnp.where(stays, near, same).astype(BF16)


def choose(at, same, near):
    out = (jax.ShapeDtypeStruct(same.shape, F32), jax.ShapeDtypeStruct(same.shape, BF16))
    return call(choose_kernel, "choose", COST_G, out, 2)(at, same, near)


def relay_kernel(at_ref, a, b, out_ref):
    out_ref[...] = (a[...].astype(F32) + b[...].astype(F32)).astype(BF16)


def relay(at, a, b):
    return call(relay_kernel, "relay", COST_R, jax.ShapeDtypeStruct(a.shape, BF16), 2)(at, a, b)


def finish_kernel(at_ref, p_ref, own, a, b, c, out_ref):
    total = own[...] + a[...].astype(F32) + b[...].astype(F32) + c[...].astype(F32)
    out_ref[...] = (p_ref[...].astype(F32) - 0.25 * total).astype(BF16)


def finish(at, params, pieces):
    out = jax.ShapeDtypeStruct(params.shape, BF16)
    return call(finish_kernel, "finish", COST_F, out, 5)(at, params, *pieces)


def gather_kernel(at_ref, alike, partner, o1, o2, o3, out_ref):
    z, c = at_ref[0], at_ref[1]
    for k in range(4):
        out_ref[k, c] = alike[k]
    for k, piece in enumerate((partner, o1, o2, o3)):
        out_ref[z ^ k, 1 - c] = piece[...]


def gather(at, alike, other):
    out = jax.ShapeDtypeStruct((4, 2) + alike.shape[1:], BF16)
    return call(gather_kernel, "gather", COST_B, out, 5)(at, alike, *other)


def arrange_kernel(at_ref, g, r1, r2, middle, edge, alike_ref, last_ref):
    z = at_ref[0]
    last = jnp.where((z == 1) | (z == 2), middle[...], edge[...])
    last_ref[...] = last
    alike_ref[z] = g[...]
    alike_ref[z ^ 1] = r1[...]
    alike_ref[z ^ 2] = r2[...]
    alike_ref[z ^ 3] = last


def arrange(at, pieces):
    shape = pieces[0].shape
    out = (jax.ShapeDtypeStruct((4,) + shape, BF16), jax.ShapeDtypeStruct(shape, BF16))
    return call(arrange_kernel, "arrange", COST_A, out, 5)(at, *pieces)


def local(grad_rows, eigen_cols, first_moment, second_moment, params, covariance):
    x, y = lax.axis_index("x"), lax.axis_index("y")
    h, z, c = lax.axis_index("zh"), lax.axis_index("zl"), lax.axis_index("c")
    vocab_total = grad_rows.shape[0] * 32

    g = grad_rows.T
    cols, rows = g.shape
    strip = cols // 4

    with jax.named_scope("early"):
        partner = flip(g, "c", 2, 1)
        across = [flip(g, "zl", 4, k) for k in (1, 2)]
        pair = jnp.where(c == 0, jnp.stack([g, partner]), jnp.stack([partner, g]))
        early = swap(jnp.broadcast_to(pair[None], (4,) + pair.shape), CROSS)
        by_rows = turn(eigen_cols.T)
        across[0], g_after, by_rows = lax.optimization_barrier((across[0], g, by_rows))
        middle = lax.ppermute(g_after, "zl", [(1, 2), (2, 1)])
        edge = lax.ppermute(across[1], "zl", [(1, 0), (2, 3)])
        alike, last = arrange(index(z), [g, *across, middle, edge])
        alike, last, early, by_rows = lax.optimization_barrier((alike, last, early, by_rows))

    with jax.named_scope("late"):
        by_strip = alike.reshape(4, 4, strip, rows)
        late = []
        for d in range(4):
            part = jnp.where(c == 0, pick(by_strip, (x + d) % 4, 1), pick(by_strip, (y + d) % 4, 0))
            if d > 0:
                part = route(
                    part,
                    lambda y, h, x, z, c: (y, h, (x + d) % 4, z, c) if c == 0 else ((y + d) % 4, h, x, z, c),
                )
            late.append(part.reshape(cols, rows))

    with jax.named_scope("cores"):
        other = [partner] + [flip(piece, "c", 2, 1) for piece in (*across, last)]
        full = gather(index(z, c), alike, other)
        flat = full.reshape(8 * cols, rows)

    with jax.named_scope("rotated"):
        rotated = lax.dot_general(
            eigen_cols, flat, (((0,), (0,)), ((), ())), preferred_element_type=F32
        )
        first_new = 0.9 * first_moment.T + 0.1 * rotated
        second_new = 0.95 * second_moment.T + 0.05 * rotated * rotated
        direction = (
            first_new / BIAS_ONE / (jnp.sqrt(second_new / BIAS_TWO) + 1e-08)
        ).astype(BF16)
        back = lax.dot_general(
            by_rows, direction, (((1,), (0,)), ((), ())), preferred_element_type=F32
        ).astype(BF16).reshape(4, 2, cols, rows)
        send = pick(back, 1 - c, 1)
        own, *both = add(index(c, z), back, flip(send, "c", 2, 1))

    with jax.named_scope("gram"):
        parts = products(index(jnp.where(c == 0, x, y), jnp.where(c == 0, y, x)), late, early)
        parts, both = lax.optimization_barrier((list(parts), both))

    with jax.named_scope("back"):
        one, two, three = both
        passed = lax.ppermute(three, "zl", [(0, 1), (3, 2)])
        middle = lax.ppermute(three, "zl", [(1, 2), (2, 1)])
        one, passed = lax.optimization_barrier((one, passed))
        two = relay(index(z), two, passed)
        got = [own, flip(one, "zl", 4, 1), flip(two, "zl", 4, 2), middle]

    with jax.named_scope("gram"):
        for d in (1, 2, 3):
            parts[d] = route(
                parts[d],
                lambda y, h, x, z, c: ((y + d) % 4, h, x, z, c) if c == 0 else (y, h, (x + d) % 4, z, c),
            )
        same, to_other = fold(index(c), parts)

    with jax.named_scope("finish"):
        params_new = finish(index(c), params.T, got)
        keep, give = choose(index(c, h), same, flip(to_other, "c", 2, 1))
        gram = keep + flip(give, "zh", 2, 1).astype(F32)
        covariance_new = 0.95 * covariance + gram * (1.0 / math.sqrt(vocab_total))
    return (params_new.T, first_new.T, second_new.T, covariance_new)


def solution(mesh):
    fine = Mesh(mesh.devices.reshape(SIZES), AXES)
    spec = P(("y", "zh", "x"), ("zl", "c"))
    return jax.shard_map(
        local,
        mesh=fine,
        in_specs=(spec, P(None, ("zl", "c")), spec, spec, spec, spec),
        out_specs=(spec, spec, spec, spec),
        check_vma=False,
    )
```

```python
import math

import jax
import jax.numpy as jnp
import numpy as np
from jax import lax
from jax.experimental import pallas as pl
from jax.experimental.pallas import tpu as pltpu
from jax.sharding import Mesh, PartitionSpec as P

BIAS_ONE = 1.0 - 0.9**10
BIAS_TWO = 1.0 - 0.95**10
BF16 = jnp.bfloat16
F32 = jnp.float32
COST_A = 16_000_000_000
COST_M = 11_000_000_000
COST_G = 1
COST_B = 10_000_000_000
COST_R = 10_000_000_000
COST_T = 1
COST_F = 20_000_000_000
AXES = ("y", "zh", "x", "zl", "c")
SIZES = (4, 2, 4, 4, 2)
IDS = np.arange(math.prod(SIZES)).reshape(SIZES)
CROSS = [r.tolist() for r in IDS[..., 0].transpose(0, 1, 3, 2).reshape(-1, 4)] + [
    r.tolist() for r in IDS[..., 1].transpose(1, 2, 3, 0).reshape(-1, 4)
]
CROSS_BACK = [r.tolist() for r in IDS[..., 0].transpose(1, 2, 3, 0).reshape(-1, 4)] + [
    r.tolist() for r in IDS[..., 1].transpose(0, 1, 3, 2).reshape(-1, 4)
]


def flip(a, axis, n, k):
    return lax.ppermute(a, axis, [(i, i ^ k) for i in range(n)])


def swap(a, groups):
    return lax.all_to_all(a, AXES, 0, 0, axis_index_groups=groups, tiled=True)


def route(a, target):
    pairs = []
    for i in range(IDS.size):
        to = target(*(int(k) for k in np.unravel_index(i, SIZES)))
        if to is not None:
            pairs.append((i, int(IDS[to])))
    return lax.ppermute(a, AXES, pairs)


def index(*at):
    return jnp.stack(at).astype(jnp.int32)


def pick(a, i, axis=0):
    return lax.dynamic_index_in_dim(a, i, axis, keepdims=False)


def spec(space=pltpu.VMEM):
    return pl.BlockSpec(memory_space=space)


def call(kernel, name, flops, out_shape, n_in, scratch=(), limit=8):
    return pl.pallas_call(
        kernel,
        out_shape=out_shape,
        in_specs=[spec(pltpu.SMEM)] + [spec()] * n_in,
        out_specs=jax.tree.map(lambda _: spec(), out_shape),
        scratch_shapes=scratch,
        compiler_params=pltpu.CompilerParams(vmem_limit_bytes=limit * 2**20),
        cost_estimate=pl.CostEstimate(flops=flops, bytes_accessed=1, transcendentals=0),
        name=name,
    )


def turn_kernel(a_ref, out_ref):
    out_ref[...] = a_ref[...].T


def turn(a):
    n, m = a.shape
    block = 1792
    return pl.pallas_call(
        turn_kernel,
        out_shape=jax.ShapeDtypeStruct((m, n), a.dtype),
        grid=(m // block,),
        in_specs=[pl.BlockSpec((n, block), lambda i: (0, i))],
        out_specs=pl.BlockSpec((block, n), lambda i: (i, 0)),
        compiler_params=pltpu.CompilerParams(vmem_limit_bytes=46 * 2**20),
        cost_estimate=pl.CostEstimate(flops=COST_T, bytes_accessed=1, transcendentals=0),
        name="turn",
    )(a)


def products_kernel(at_ref, l0, l1, l2, l3, early_ref, o0, o1, o2, o3, held):
    me, to = at_ref[0], at_ref[1]
    strip = held.shape[1]
    left = jnp.concatenate([l0[...], l1[...], l2[...], l3[...]], axis=1)
    for w in range(2):
        right = jnp.concatenate([early_ref[(me - d + 4) % 4, w] for d in range(4)], axis=1)
        total = lax.dot_general(
            left, right, (((1,), (1,)), ((), ())), preferred_element_type=F32
        )
        for j in range(4):
            held[j] = total[j * strip : (j + 1) * strip]
        for d, out in enumerate((o0, o1, o2, o3)):
            out[w] = held[(to + d) % 4].astype(BF16)


def products(at, late, early):
    cols = late[0].shape[0]
    out = jax.ShapeDtypeStruct((2, cols // 4, cols), BF16)
    held = pltpu.VMEM((4, cols // 4, cols), F32)
    return call(products_kernel, "products", COST_M, (out,) * 4, 5, [held], limit=20)(at, *late, early)


def add_kernel(at_ref, back_ref, got_ref, own_ref, *outs):
    c, z = at_ref[0], at_ref[1]
    total = [None] * 4
    for k in range(4):
        to = z ^ k
        value = back_ref[to, c].astype(F32) + got_ref[to].astype(F32)
        if k == 0:
            own_ref[...] = value
        else:
            outs[k - 1][...] = value.astype(BF16)


def add(at, back, got):
    shape = got.shape[1:]
    out = (jax.ShapeDtypeStruct(shape, F32),) + (jax.ShapeDtypeStruct(shape, BF16),) * 3
    return call(add_kernel, "add", 1, out, 2)(at, back, got)


def fold_kernel(at_ref, a, b, c, d, same_ref, other_ref):
    first = at_ref[0] == 0
    even = sum(r[0].astype(F32) for r in (a, b, c, d))
    odd = sum(r[1].astype(F32) for r in (a, b, c, d))
    same_ref[...] = jnp.where(first, even, odd)
    other_ref[...] = jnp.where(first, odd, even).astype(BF16)


def fold(at, parts):
    shape = parts[0].shape[1:]
    out = (jax.ShapeDtypeStruct(shape, F32), jax.ShapeDtypeStruct(shape, BF16))
    return call(fold_kernel, "fold", COST_G, out, 4)(at, *parts)


def choose_kernel(at_ref, same_ref, near_ref, keep_ref, give_ref):
    stays = at_ref[0] == at_ref[1]
    same, near = same_ref[...], near_ref[...].astype(F32)
    keep_ref[...] = jnp.where(stays, same, near)
    give_ref[...] = jnp.where(stays, near, same).astype(BF16)


def choose(at, same, near):
    out = (jax.ShapeDtypeStruct(same.shape, F32), jax.ShapeDtypeStruct(same.shape, BF16))
    return call(choose_kernel, "choose", COST_G, out, 2)(at, same, near)


def relay_kernel(at_ref, a, b, out_ref):
    out_ref[...] = (a[...].astype(F32) + b[...].astype(F32)).astype(BF16)


def relay(at, a, b):
    return call(relay_kernel, "relay", COST_R, jax.ShapeDtypeStruct(a.shape, BF16), 2)(at, a, b)


def finish_kernel(at_ref, p_ref, own, a, b, c, out_ref):
    total = own[...] + a[...].astype(F32) + b[...].astype(F32) + c[...].astype(F32)
    out_ref[...] = (p_ref[...].astype(F32) - 0.25 * total).astype(BF16)


def finish(at, params, pieces):
    out = jax.ShapeDtypeStruct(params.shape, BF16)
    return call(finish_kernel, "finish", COST_F, out, 5)(at, params, *pieces)


def gather_kernel(at_ref, alike, partner, o1, o2, o3, out_ref):
    z, c = at_ref[0], at_ref[1]
    for k in range(4):
        out_ref[k, c] = alike[k]
    for k, piece in enumerate((partner, o1, o2, o3)):
        out_ref[z ^ k, 1 - c] = piece[...]


def gather(at, alike, other):
    out = jax.ShapeDtypeStruct((4, 2) + alike.shape[1:], BF16)
    return call(gather_kernel, "gather", COST_B, out, 5)(at, alike, *other)


def arrange_kernel(at_ref, g, r1, r2, middle, edge, alike_ref, last_ref):
    z = at_ref[0]
    last = jnp.where((z == 1) | (z == 2), middle[...], edge[...])
    last_ref[...] = last
    alike_ref[z] = g[...]
    alike_ref[z ^ 1] = r1[...]
    alike_ref[z ^ 2] = r2[...]
    alike_ref[z ^ 3] = last


def arrange(at, pieces):
    shape = pieces[0].shape
    out = (jax.ShapeDtypeStruct((4,) + shape, BF16), jax.ShapeDtypeStruct(shape, BF16))
    return call(arrange_kernel, "arrange", COST_A, out, 5)(at, *pieces)


def local(grad_rows, eigen_cols, first_moment, second_moment, params, covariance):
    x, y = lax.axis_index("x"), lax.axis_index("y")
    h, z, c = lax.axis_index("zh"), lax.axis_index("zl"), lax.axis_index("c")
    vocab_total = grad_rows.shape[0] * 32

    g = grad_rows.T
    cols, rows = g.shape
    strip = cols // 4

    with jax.named_scope("early"):
        partner = flip(g, "c", 2, 1)
        across = [flip(g, "zl", 4, k) for k in (1, 2)]
        pair = jnp.where(c == 0, jnp.stack([g, partner]), jnp.stack([partner, g]))
        early = swap(jnp.broadcast_to(pair[None], (4,) + pair.shape), CROSS)
        by_rows = turn(eigen_cols.T)
        across[0], g_after, by_rows = lax.optimization_barrier((across[0], g, by_rows))
        middle = lax.ppermute(g_after, "zl", [(1, 2), (2, 1)])
        edge = lax.ppermute(across[1], "zl", [(1, 0), (2, 3)])
        alike, last = arrange(index(z), [g, *across, middle, edge])
        alike, last, early, by_rows = lax.optimization_barrier((alike, last, early, by_rows))

    with jax.named_scope("late"):
        by_strip = alike.reshape(4, 4, strip, rows)
        late = []
        for d in range(4):
            part = jnp.where(c == 0, pick(by_strip, (x + d) % 4, 1), pick(by_strip, (y + d) % 4, 0))
            if d > 0:
                part = route(
                    part,
                    lambda y, h, x, z, c: (y, h, (x + d) % 4, z, c) if c == 0 else ((y + d) % 4, h, x, z, c),
                )
            late.append(part.reshape(cols, rows))

    with jax.named_scope("cores"):
        other = [partner] + [flip(piece, "c", 2, 1) for piece in (*across, last)]
        full = gather(index(z, c), alike, other)
        flat = full.reshape(8 * cols, rows)

    with jax.named_scope("rotated"):
        rotated = lax.dot_general(
            eigen_cols, flat, (((0,), (0,)), ((), ())), preferred_element_type=F32
        )
        first_new = 0.9 * first_moment.T + 0.1 * rotated
        second_new = 0.95 * second_moment.T + 0.05 * rotated * rotated
        direction = (
            first_new / BIAS_ONE / (jnp.sqrt(second_new / BIAS_TWO) + 1e-08)
        ).astype(BF16)
        back = lax.dot_general(
            by_rows, direction, (((1,), (0,)), ((), ())), preferred_element_type=F32
        ).astype(BF16).reshape(4, 2, cols, rows)
        send = pick(back, 1 - c, 1)
        own, *both = add(index(c, z), back, flip(send, "c", 2, 1))

    with jax.named_scope("gram"):
        parts = products(index(jnp.where(c == 0, x, y), jnp.where(c == 0, y, x)), late, early)
        parts, both = lax.optimization_barrier((list(parts), both))

    with jax.named_scope("back"):
        one, two, three = both
        passed = lax.ppermute(three, "zl", [(0, 1), (3, 2)])
        middle = lax.ppermute(three, "zl", [(1, 2), (2, 1)])
        two = relay(index(z), two, passed)
        one, passed, middle = lax.optimization_barrier((one, passed, middle))
        got = [own, flip(one, "zl", 4, 1), flip(two, "zl", 4, 2), middle]

    with jax.named_scope("gram"):
        for d in (1, 2, 3):
            parts[d] = route(
                parts[d],
                lambda y, h, x, z, c: ((y + d) % 4, h, x, z, c) if c == 0 else (y, h, (x + d) % 4, z, c),
            )
        same, to_other = fold(index(c), parts)

    with jax.named_scope("finish"):
        params_new = finish(index(c), params.T, got)
        keep, give = choose(index(c, h), same, flip(to_other, "c", 2, 1))
        gram = keep + flip(give, "zh", 2, 1).astype(F32)
        covariance_new = 0.95 * covariance + gram * (1.0 / math.sqrt(vocab_total))
    return (params_new.T, first_new.T, second_new.T, covariance_new)


def solution(mesh):
    fine = Mesh(mesh.devices.reshape(SIZES), AXES)
    spec = P(("y", "zh", "x"), ("zl", "c"))
    return jax.shard_map(
        local,
        mesh=fine,
        in_specs=(spec, P(None, ("zl", "c")), spec, spec, spec, spec),
        out_specs=(spec, spec, spec, spec),
        check_vma=False,
    )
```

```python
import math

import jax
import jax.numpy as jnp
import numpy as np
from jax import lax
from jax.experimental import pallas as pl
from jax.experimental.pallas import tpu as pltpu
from jax.sharding import Mesh, PartitionSpec as P

BIAS_ONE = 1.0 - 0.9**10
BIAS_TWO = 1.0 - 0.95**10
BF16 = jnp.bfloat16
F32 = jnp.float32
COST_A = 16_000_000_000
COST_M = 11_000_000_000
COST_G = 1
COST_B = 10_000_000_000
COST_R = 10_000_000_000
COST_T = 1
COST_F = 20_000_000_000
AXES = ("y", "zh", "x", "zl", "c")
SIZES = (4, 2, 4, 4, 2)
IDS = np.arange(math.prod(SIZES)).reshape(SIZES)
CROSS = [r.tolist() for r in IDS[..., 0].transpose(0, 1, 3, 2).reshape(-1, 4)] + [
    r.tolist() for r in IDS[..., 1].transpose(1, 2, 3, 0).reshape(-1, 4)
]
CROSS_BACK = [r.tolist() for r in IDS[..., 0].transpose(1, 2, 3, 0).reshape(-1, 4)] + [
    r.tolist() for r in IDS[..., 1].transpose(0, 1, 3, 2).reshape(-1, 4)
]


def flip(a, axis, n, k):
    return lax.ppermute(a, axis, [(i, i ^ k) for i in range(n)])


def swap(a, groups):
    return lax.all_to_all(a, AXES, 0, 0, axis_index_groups=groups, tiled=True)


def route(a, target):
    pairs = []
    for i in range(IDS.size):
        to = target(*(int(k) for k in np.unravel_index(i, SIZES)))
        if to is not None:
            pairs.append((i, int(IDS[to])))
    return lax.ppermute(a, AXES, pairs)


def index(*at):
    return jnp.stack(at).astype(jnp.int32)


def pick(a, i, axis=0):
    return lax.dynamic_index_in_dim(a, i, axis, keepdims=False)


def spec(space=pltpu.VMEM):
    return pl.BlockSpec(memory_space=space)


def call(kernel, name, flops, out_shape, n_in, scratch=(), limit=7):
    return pl.pallas_call(
        kernel,
        out_shape=out_shape,
        in_specs=[spec(pltpu.SMEM)] + [spec()] * n_in,
        out_specs=jax.tree.map(lambda _: spec(), out_shape),
        scratch_shapes=scratch,
        compiler_params=pltpu.CompilerParams(vmem_limit_bytes=limit * 2**20),
        cost_estimate=pl.CostEstimate(flops=flops, bytes_accessed=1, transcendentals=0),
        name=name,
    )


def turn_kernel(a_ref, out_ref):
    out_ref[...] = a_ref[...].T


def turn(a):
    n, m = a.shape
    block = 1792
    return pl.pallas_call(
        turn_kernel,
        out_shape=jax.ShapeDtypeStruct((m, n), a.dtype),
        grid=(m // block,),
        in_specs=[pl.BlockSpec((n, block), lambda i: (0, i))],
        out_specs=pl.BlockSpec((block, n), lambda i: (i, 0)),
        compiler_params=pltpu.CompilerParams(vmem_limit_bytes=46 * 2**20),
        cost_estimate=pl.CostEstimate(flops=COST_T, bytes_accessed=1, transcendentals=0),
        name="turn",
    )(a)


def products_kernel(at_ref, l0, l1, l2, l3, early_ref, o0, o1, o2, o3, held):
    me, to = at_ref[0], at_ref[1]
    strip = held.shape[1]
    left = jnp.concatenate([l0[...], l1[...], l2[...], l3[...]], axis=1)
    for w in range(2):
        right = jnp.concatenate([early_ref[(me - d + 4) % 4, w] for d in range(4)], axis=1)
        total = lax.dot_general(
            left, right, (((1,), (1,)), ((), ())), preferred_element_type=F32
        )
        for j in range(4):
            held[j] = total[j * strip : (j + 1) * strip]
        for d, out in enumerate((o0, o1, o2, o3)):
            out[w] = held[(to + d) % 4].astype(BF16)


def products(at, late, early):
    cols = late[0].shape[0]
    out = jax.ShapeDtypeStruct((2, cols // 4, cols), BF16)
    held = pltpu.VMEM((4, cols // 4, cols), F32)
    return call(products_kernel, "products", COST_M, (out,) * 4, 5, [held], limit=16)(at, *late, early)


def add_kernel(at_ref, back_ref, got_ref, own_ref, *outs):
    c, z = at_ref[0], at_ref[1]
    total = [None] * 4
    for k in range(4):
        to = z ^ k
        value = back_ref[to, c].astype(F32) + got_ref[to].astype(F32)
        if k == 0:
            own_ref[...] = value
        else:
            outs[k - 1][...] = value.astype(BF16)


def add(at, back, got):
    shape = got.shape[1:]
    out = (jax.ShapeDtypeStruct(shape, F32),) + (jax.ShapeDtypeStruct(shape, BF16),) * 3
    return call(add_kernel, "add", 1, out, 2)(at, back, got)


def fold_kernel(at_ref, a, b, c, d, same_ref, other_ref):
    first = at_ref[0] == 0
    even = sum(r[0].astype(F32) for r in (a, b, c, d))
    odd = sum(r[1].astype(F32) for r in (a, b, c, d))
    same_ref[...] = jnp.where(first, even, odd)
    other_ref[...] = jnp.where(first, odd, even).astype(BF16)


def fold(at, parts):
    shape = parts[0].shape[1:]
    out = (jax.ShapeDtypeStruct(shape, F32), jax.ShapeDtypeStruct(shape, BF16))
    return call(fold_kernel, "fold", COST_G, out, 4)(at, *parts)


def choose_kernel(at_ref, same_ref, near_ref, keep_ref, give_ref):
    stays = at_ref[0] == at_ref[1]
    same, near = same_ref[...], near_ref[...].astype(F32)
    keep_ref[...] = jnp.where(stays, same, near)
    give_ref[...] = jnp.where(stays, near, same).astype(BF16)


def choose(at, same, near):
    out = (jax.ShapeDtypeStruct(same.shape, F32), jax.ShapeDtypeStruct(same.shape, BF16))
    return call(choose_kernel, "choose", COST_G, out, 2)(at, same, near)


def relay_kernel(at_ref, a, b, out_ref):
    out_ref[...] = (a[...].astype(F32) + b[...].astype(F32)).astype(BF16)


def relay(at, a, b):
    return call(relay_kernel, "relay", COST_R, jax.ShapeDtypeStruct(a.shape, BF16), 2)(at, a, b)


def finish_kernel(at_ref, p_ref, own, a, b, c, out_ref):
    total = own[...] + a[...].astype(F32) + b[...].astype(F32) + c[...].astype(F32)
    out_ref[...] = (p_ref[...].astype(F32) - 0.25 * total).astype(BF16)


def finish(at, params, pieces):
    out = jax.ShapeDtypeStruct(params.shape, BF16)
    return call(finish_kernel, "finish", COST_F, out, 5)(at, params, *pieces)


def gather_kernel(at_ref, alike, partner, o1, o2, o3, out_ref):
    z, c = at_ref[0], at_ref[1]
    for k in range(4):
        out_ref[k, c] = alike[k]
    for k, piece in enumerate((partner, o1, o2, o3)):
        out_ref[z ^ k, 1 - c] = piece[...]


def gather(at, alike, other):
    out = jax.ShapeDtypeStruct((4, 2) + alike.shape[1:], BF16)
    return call(gather_kernel, "gather", COST_B, out, 5)(at, alike, *other)


def arrange_kernel(at_ref, g, r1, r2, middle, edge, alike_ref, last_ref):
    z = at_ref[0]
    last = jnp.where((z == 1) | (z == 2), middle[...], edge[...])
    last_ref[...] = last
    alike_ref[z] = g[...]
    alike_ref[z ^ 1] = r1[...]
    alike_ref[z ^ 2] = r2[...]
    alike_ref[z ^ 3] = last


def arrange(at, pieces):
    shape = pieces[0].shape
    out = (jax.ShapeDtypeStruct((4,) + shape, BF16), jax.ShapeDtypeStruct(shape, BF16))
    return call(arrange_kernel, "arrange", COST_A, out, 5)(at, *pieces)


def local(grad_rows, eigen_cols, first_moment, second_moment, params, covariance):
    x, y = lax.axis_index("x"), lax.axis_index("y")
    h, z, c = lax.axis_index("zh"), lax.axis_index("zl"), lax.axis_index("c")
    vocab_total = grad_rows.shape[0] * 32

    g = grad_rows.T
    cols, rows = g.shape
    strip = cols // 4

    with jax.named_scope("early"):
        partner = flip(g, "c", 2, 1)
        across = [flip(g, "zl", 4, k) for k in (1, 2)]
        pair = jnp.where(c == 0, jnp.stack([g, partner]), jnp.stack([partner, g]))
        early = swap(jnp.broadcast_to(pair[None], (4,) + pair.shape), CROSS)
        by_rows = turn(eigen_cols.T)
        across[0], g_after, by_rows = lax.optimization_barrier((across[0], g, by_rows))
        middle = lax.ppermute(g_after, "zl", [(1, 2), (2, 1)])
        edge = lax.ppermute(across[1], "zl", [(1, 0), (2, 3)])
        alike, last = arrange(index(z), [g, *across, middle, edge])
        alike, last, early, by_rows = lax.optimization_barrier((alike, last, early, by_rows))

    with jax.named_scope("late"):
        by_strip = alike.reshape(4, 4, strip, rows)
        late = []
        for d in range(4):
            part = jnp.where(c == 0, pick(by_strip, (x + d) % 4, 1), pick(by_strip, (y + d) % 4, 0))
            if d > 0:
                part = route(
                    part,
                    lambda y, h, x, z, c: (y, h, (x + d) % 4, z, c) if c == 0 else ((y + d) % 4, h, x, z, c),
                )
            late.append(part.reshape(cols, rows))

    with jax.named_scope("cores"):
        other = [partner] + [flip(piece, "c", 2, 1) for piece in (*across, last)]
        full = gather(index(z, c), alike, other)
        flat = full.reshape(8 * cols, rows)

    with jax.named_scope("rotated"):
        rotated = lax.dot_general(
            eigen_cols, flat, (((0,), (0,)), ((), ())), preferred_element_type=F32
        )
        first_new = 0.9 * first_moment.T + 0.1 * rotated
        second_new = 0.95 * second_moment.T + 0.05 * rotated * rotated
        direction = (
            first_new / BIAS_ONE / (jnp.sqrt(second_new / BIAS_TWO) + 1e-08)
        ).astype(BF16)
        back = lax.dot_general(
            by_rows, direction, (((1,), (0,)), ((), ())), preferred_element_type=F32
        ).astype(BF16).reshape(4, 2, cols, rows)
        send = pick(back, 1 - c, 1)
        own, *both = add(index(c, z), back, flip(send, "c", 2, 1))

    with jax.named_scope("gram"):
        parts = products(index(jnp.where(c == 0, x, y), jnp.where(c == 0, y, x)), late, early)
        parts, both = lax.optimization_barrier((list(parts), both))

    with jax.named_scope("back"):
        one, two, three = both
        passed = lax.ppermute(three, "zl", [(0, 1), (3, 2)])
        middle = lax.ppermute(three, "zl", [(1, 2), (2, 1)])
        two = relay(index(z), two, passed)
        one, passed, middle = lax.optimization_barrier((one, passed, middle))
        got = [own, flip(one, "zl", 4, 1), flip(two, "zl", 4, 2), middle]

    with jax.named_scope("gram"):
        for d in (1, 2, 3):
            parts[d] = route(
                parts[d],
                lambda y, h, x, z, c: ((y + d) % 4, h, x, z, c) if c == 0 else (y, h, (x + d) % 4, z, c),
            )
        same, to_other = fold(index(c), parts)

    with jax.named_scope("finish"):
        params_new = finish(index(c), params.T, got)
        keep, give = choose(index(c, h), same, flip(to_other, "c", 2, 1))
        gram = keep + flip(give, "zh", 2, 1).astype(F32)
        covariance_new = 0.95 * covariance + gram * (1.0 / math.sqrt(vocab_total))
    return (params_new.T, first_new.T, second_new.T, covariance_new)


def solution(mesh):
    fine = Mesh(mesh.devices.reshape(SIZES), AXES)
    spec = P(("y", "zh", "x"), ("zl", "c"))
    return jax.shard_map(
        local,
        mesh=fine,
        in_specs=(spec, P(None, ("zl", "c")), spec, spec, spec, spec),
        out_specs=(spec, spec, spec, spec),
        check_vma=False,
    )
```
